32 devices in a mesh: replica: 8 (over z, x), tensor: 4 (over y, core).
Axes of the slice: x: 2, y: 2, z: 4, core: 2. Of those that a mesh axis runs over, the one named last changes fastest.
Arguments:
- tokens: bfloat16 [8, 384, 2048], P('replica', 'tensor'), may hold values from -6 to 6
- targets: bfloat16 [8, 384, 2048], P('replica', 'tensor'), may hold values from -6 to 6
- gate_weight: bfloat16 [8, 2048, 7168], P('replica', None, 'tensor'), may hold values from -6 to 6
- probes: bfloat16 [8, 2048, 7168], P('replica', None, 'tensor'), may hold values from -6 to 6
- tracker: bfloat16 [8, 2048, 7168], P('replica', None, 'tensor'), may hold values from 0.049804688 to 2
- up_weight: bfloat16 [2048, 7168], P('replica', 'tensor'), may hold values from -6 to 6
- down_weight: bfloat16 [7168, 2048], P('tensor', 'replica'), may hold values from -6 to 6
- neighbours: int32 [8, 6], replicated, may hold values from 0 to 7, as said below
- numerators: int32 [8, 6], replicated, may hold values from 0 to 8, as said below
Outputs:
- mixed_weights: bfloat16 [8, 2048, 7168], P('replica', None, 'tensor')
- mixed_tracker: bfloat16 [8, 2048, 7168], P('replica', None, 'tensor')
The draws below stay inside these ranges and needn't reach their ends.
Inputs may be any that keep to these rules, and one draw needn't show every extreme that they name: `neighbours`: every slot of row r holds r itself or a replica r - o modulo 8 with o one of 1, -1, 2, -2, 4, -4, each o at most once in a row; a row has between 2 and 6 slots that are not r, and some row has 6. `numerators`: A numerator is 0 exactly in slots that hold the row's own replica, and 4 to 8 elsewhere.
All inputs are finite; a program needn't handle non-finite values.
Results may differ from the reference program's by a relative error of at most 0.0058.
Values may be sent and summed in bfloat16 or wider, within the bound.
No kernel may reach another device: no remote copies, remote signals or barrier semaphores. Data moves between devices by JAX's collectives and lax.ppermute only.
A program may use at most 192 MiB of HBM per device.

```python
import math
import jax
import jax.numpy as jnp

D = 2048
FF = 7168
TOK = 384
DEG = 6
DEN = 64
REPLICAS = 8


def graph_pattern(key):
    keys = jax.random.split(key, 5)
    row_ids = jnp.arange(REPLICAS, dtype=jnp.int32)
    degrees = jax.random.randint(keys[0], (REPLICAS,), 2, DEG + 1)
    end_rows = (row_ids == 0) | (row_ids == REPLICAS - 1)
    degrees = jnp.where(end_rows, jnp.minimum(degrees, DEG - 1), degrees)
    busiest = jax.random.randint(keys[1], (), 1, REPLICAS - 1)
    sparsest = (busiest + 1 + jax.random.randint(keys[2], (), 0, REPLICAS - 1)) % REPLICAS
    degrees = jnp.where(row_ids == busiest, DEG, jnp.where(row_ids == sparsest, 2, degrees))
    scores = jax.random.randint(keys[3], (REPLICAS, 6), 0, 1 << 20) * 8 + jnp.arange(6, dtype=jnp.int32)[None, :]
    order = jnp.argsort(scores, axis=1)
    table = jnp.array([1, -1, 2, -2, 4, -4], dtype=jnp.int32)
    offsets = table[order][:, :DEG]
    slots = jnp.arange(DEG, dtype=jnp.int32)
    live = slots[None, :] < degrees[:, None]
    linked = jnp.where(live, jnp.mod(row_ids[:, None] - offsets, REPLICAS), row_ids[:, None])
    weights = jnp.where(live, jax.random.randint(keys[4], (REPLICAS, DEG), 4, 9), 0)
    weights = weights.at[busiest, 0].set(8)
    return (linked.astype(jnp.int32), weights.astype(jnp.int32))


def draw_neighbours(key, part):
    linked, weights = graph_pattern(key)
    return linked


def draw_numerators(key, part):
    linked, weights = graph_pattern(key)
    return weights


def level_of(key, shape, pieces, smallest, top_value):
    gain, own = 1.0, jax.random.fold_in(key, 6)
    for axis_at, shards_of in pieces:
        draws = jnp.exp(jax.random.uniform(jax.random.fold_in(own, axis_at), (shards_of,), jnp.float32, smallest / len(pieces), top_value / len(pieces)))
        gain = gain * jnp.repeat(draws, shape[axis_at] // shards_of).reshape([-1 if axis == axis_at else 1 for axis in range(len(shape))])
    return gain


def centred(own_key, dims, width, limit, cuts=(), kind=jnp.bfloat16):
    gain = level_of(own_key, dims, cuts, -0.22, 0.18) if cuts else 1.0
    values = jax.random.normal(own_key, dims, jnp.float32) * width * gain
    return jnp.minimum(jnp.maximum(values, -limit), limit).astype(kind)


def setup_inputs(seed: int = 0) -> dict:
    key_of = jax.random.split(jax.random.key(seed), 10)
    return {
        "tokens": centred(key_of[0], (REPLICAS, TOK, D), 1.0, 6.0, ((0, 8), (1, 4))),
        "targets": centred(key_of[1], (REPLICAS, TOK, D), 1.0, 6.0, ((0, 8), (1, 4))),
        "gate_weight": centred(key_of[2], (REPLICAS, D, FF), 1.0, 6.0, ((0, 8), (2, 4))),
        "probes": centred(key_of[3], (REPLICAS, D, FF), 1.0, 6.0, ((0, 8), (2, 4))),
        "tracker": jnp.clip(jnp.exp(math.log(2.0) - 3.6927934 * jax.random.uniform(key_of[4], (REPLICAS, D, FF), jnp.float32) ** level_of(key_of[4], (REPLICAS, D, FF), ((0, 8), (2, 4)), -0.2, 0.2)), 0.049804688, 2.0).astype(jnp.bfloat16),
        "up_weight": centred(key_of[5], (D, FF), 1.0, 6.0, ((0, 8), (1, 4))),
        "down_weight": centred(key_of[6], (FF, D), 1.0, 6.0, ((0, 4), (1, 8))),
        "neighbours": draw_neighbours(jax.random.fold_in(key_of[9], 71), 0),
        "numerators": draw_numerators(jax.random.fold_in(key_of[9], 71), 0),
    }


step_size = 0.1
floor_value = 0.1
tracker_decay = 0.75

def derivatives(gate_pre):
    logistic = jax.nn.sigmoid(gate_pre)
    activated = gate_pre * logistic
    slope_one = logistic * (1.0 + gate_pre * (1.0 - logistic))
    slope_two = logistic * (1.0 - logistic) * (2.0 + gate_pre * (1.0 - 2.0 * logistic))
    return (activated, slope_one, slope_two)

def replica_pass(tokens_one, targets_one, weight_now, probe, tracker_now, up_weight, down_weight):
    inv_width = 1.0 / math.sqrt(D)
    inv_hidden = 1.0 / math.sqrt(FF)
    gate_pre = jnp.dot(tokens_one, weight_now, preferred_element_type=jnp.float32) * inv_width
    up_pre = jnp.dot(tokens_one, up_weight, preferred_element_type=jnp.float32) * inv_width
    activated, slope_one, slope_two = derivatives(gate_pre)
    hidden = (activated * up_pre).astype(jnp.bfloat16)
    outputs = jnp.dot(hidden, down_weight, preferred_element_type=jnp.float32) * inv_hidden
    residual = (outputs - targets_one.astype(jnp.float32)).astype(jnp.bfloat16)
    grad_hidden = jnp.dot(residual, down_weight.T, preferred_element_type=jnp.float32) * inv_hidden
    grad_gate = (grad_hidden * up_pre * slope_one).astype(jnp.bfloat16)
    gradient = jnp.dot(tokens_one.T, grad_gate, preferred_element_type=jnp.float32) * inv_width
    ratio = gradient / jnp.maximum(tracker_now.astype(jnp.float32), floor_value)
    stepped = (weight_now.astype(jnp.float32) - step_size * jnp.clip(ratio, -1.0, 1.0)).astype(jnp.bfloat16)
    probe_pre = jnp.dot(tokens_one, probe, preferred_element_type=jnp.float32) * inv_width
    tangent_hidden = (slope_one * probe_pre * up_pre).astype(jnp.bfloat16)
    tangent_out = jnp.dot(tangent_hidden, down_weight, preferred_element_type=jnp.float32) * inv_hidden
    tangent_res = tangent_out.astype(jnp.bfloat16)
    tangent_grad = jnp.dot(tangent_res, down_weight.T, preferred_element_type=jnp.float32) * inv_hidden
    tangent_gate = ((tangent_grad * slope_one + grad_hidden * slope_two * probe_pre) * up_pre).astype(jnp.bfloat16)
    curvature_probe = jnp.dot(tokens_one.T, tangent_gate, preferred_element_type=jnp.float32) * inv_width
    tracked = (tracker_decay * tracker_now.astype(jnp.float32) + (1.0 - tracker_decay) * probe.astype(jnp.float32) * curvature_probe).astype(jnp.bfloat16)
    return (stepped, tracked)

def mix_all(stacked, neighbours, numerators):
    mixed_rows = []
    for replica in range(REPLICAS):
        self_weight = (DEN - jnp.sum(numerators[replica])).astype(jnp.float32) / DEN
        mixed_sum = self_weight * stacked[replica].astype(jnp.float32)
        for slot in range(DEG):
            share = numerators[replica, slot].astype(jnp.float32) / DEN
            mixed_sum = mixed_sum + share * stacked[neighbours[replica, slot]].astype(jnp.float32)
        mixed_rows.append(mixed_sum.astype(jnp.bfloat16))
    return jnp.stack(mixed_rows)

def reference(tokens, targets, gate_weight, probes, tracker, up_weight, down_weight, neighbours, numerators):
    stepped_rows = []
    tracked_rows = []
    for replica in range(REPLICAS):
        stepped, tracked = replica_pass(tokens[replica], targets[replica], gate_weight[replica], probes[replica], tracker[replica], up_weight, down_weight)
        stepped_rows.append(stepped)
        tracked_rows.append(tracked)
    mixed_weights = mix_all(jnp.stack(stepped_rows), neighbours, numerators)
    mixed_tracker = mix_all(jnp.stack(tracked_rows), neighbours, numerators)
    return (mixed_weights, mixed_tracker)
```

```python
import functools
import math

import jax
import jax.numpy as jnp
import numpy as np
from jax import lax
from jax.experimental import pallas as pl
from jax.experimental.pallas import tpu as pltpu
from jax.sharding import PartitionSpec as P

DEN = 64

step_size = 0.1
floor_value = 0.1
tracker_decay = 0.75

VMEM_BYTES = 40 * 1024 * 1024


def send(value, pairs):
    return lax.ppermute(value, "replica", pairs)


def step_body(inv_width, xt_ref, grad_ref, weight_ref, tracker_ref, out_ref):
    gradient = jnp.dot(xt_ref[...], grad_ref[...], preferred_element_type=jnp.float32) * inv_width
    ratio = gradient / jnp.maximum(tracker_ref[...].astype(jnp.float32), floor_value)
    out_ref[...] = (
        weight_ref[...].astype(jnp.float32) - step_size * jnp.clip(ratio, -1.0, 1.0)
    ).astype(out_ref.dtype)


def track_body(inv_width, xt_ref, grad_ref, probe_ref, tracker_ref, out_ref):
    curvature = jnp.dot(xt_ref[...], grad_ref[...], preferred_element_type=jnp.float32) * inv_width
    out_ref[...] = (
        tracker_decay * tracker_ref[...].astype(jnp.float32)
        + (1.0 - tracker_decay) * probe_ref[...].astype(jnp.float32) * curvature
    ).astype(out_ref.dtype)


def update_rows(body, name, tokens_t, grads, first, second):
    rows, width = first.shape
    depth = grads.shape[0]
    size = min(rows, 256)
    row_spec = pl.BlockSpec((size, width), lambda i: (i, 0))
    return pl.pallas_call(
        functools.partial(body, 1.0 / math.sqrt(rows)),
        grid=(rows // size,),
        in_specs=[
            pl.BlockSpec((size, depth), lambda i: (i, 0)),
            pl.BlockSpec((depth, width), lambda i: (0, 0)),
            row_spec,
            row_spec,
        ],
        out_specs=row_spec,
        out_shape=jax.ShapeDtypeStruct((rows, width), jnp.bfloat16),
        compiler_params=pltpu.CompilerParams(vmem_limit_bytes=VMEM_BYTES),
        name=name,
    )(tokens_t, grads, first, second)


def weighted_body(count, scale_ref, *refs):
    total = scale_ref[0] * refs[0][...].astype(jnp.float32)
    for k in range(1, count):
        total = total + scale_ref[k] * refs[k][...].astype(jnp.float32)
    refs[-1][...] = total.astype(refs[-1].dtype)


def weighted_sum(name, scales, parts):
    rows, width = parts[0].shape
    size = min(rows, 128)
    row_spec = pl.BlockSpec((size, width), lambda i: (i, 0))
    return pl.pallas_call(
        functools.partial(weighted_body, len(parts)),
        grid=(rows // size,),
        in_specs=[pl.BlockSpec(memory_space=pltpu.SMEM)] + [row_spec] * len(parts),
        out_specs=row_spec,
        out_shape=jax.ShapeDtypeStruct((rows, width), jnp.bfloat16),
        compiler_params=pltpu.CompilerParams(vmem_limit_bytes=VMEM_BYTES),
        name=name,
    )(scales, *parts)


def after(value, *earlier):
    def body(value_ref, *refs):
        refs[-1][...] = value_ref[...]

    return pl.pallas_call(
        body,
        in_specs=[pl.BlockSpec(memory_space=pltpu.VMEM)]
        + [pl.BlockSpec(memory_space=pl.ANY)] * len(earlier),
        out_specs=pl.BlockSpec(memory_space=pltpu.VMEM),
        out_shape=jax.ShapeDtypeStruct(value.shape, value.dtype),
        compiler_params=pltpu.CompilerParams(vmem_limit_bytes=VMEM_BYTES),
        name="after",
    )(value, *earlier)


def blank(shape, dtype):
    def body(out_ref):
        pass

    return pl.pallas_call(
        body,
        out_specs=pl.BlockSpec(memory_space=pl.ANY),
        out_shape=jax.ShapeDtypeStruct(shape, dtype),
        name="blank",
    )()


def by_rows(body, name, results, *operands):
    rows, width = operands[0].shape
    size = rows // 4 if rows % 64 == 0 else rows
    row_spec = pl.BlockSpec((size, width), lambda i: (i, 0))
    return pl.pallas_call(
        body,
        grid=(rows // size,),
        in_specs=[row_spec] * len(operands),
        out_specs=[row_spec] * len(results),
        out_shape=[jax.ShapeDtypeStruct((rows, width), kind) for kind in results],
        compiler_params=pltpu.CompilerParams(vmem_limit_bytes=VMEM_BYTES),
        name=name,
    )(*operands)


def chip_sum_body(mine_ref, theirs_ref, sum_ref, sent_ref):
    total = mine_ref[...] + theirs_ref[...]
    sum_ref[...] = total
    sent_ref[...] = total.astype(sent_ref.dtype)


def residual_body(chip_ref, beyond_ref, target_ref, out_ref):
    total = chip_ref[...] + beyond_ref[...].astype(jnp.float32)
    out_ref[...] = (total - target_ref[...].astype(jnp.float32)).astype(out_ref.dtype)


def tangent_body(chip_ref, beyond_ref, out_ref):
    total = chip_ref[...] + beyond_ref[...].astype(jnp.float32)
    out_ref[...] = total.astype(out_ref.dtype)


def turned(value):
    rows, width = value.shape
    size = 256

    def body(value_ref, out_ref):
        out_ref[...] = value_ref[...].T

    return pl.pallas_call(
        body,
        grid=(width // size,),
        in_specs=[pl.BlockSpec((rows, size), lambda i: (0, i))],
        out_specs=pl.BlockSpec((size, rows), lambda i: (i, 0)),
        out_shape=jax.ShapeDtypeStruct((width, rows), value.dtype),
        compiler_params=pltpu.CompilerParams(vmem_limit_bytes=VMEM_BYTES),
        name="turned",
    )(value)


def half_rows(*arrays):
    beyond = lax.ppermute(
        jnp.concatenate(arrays, axis=0), "tensor", [(0, 2), (2, 0), (1, 3), (3, 1)]
    )
    first = lax.axis_index("tensor") < 2
    found = []
    for rows, other in zip(arrays, jnp.split(beyond, len(arrays), axis=0)):
        found.append(
            jnp.concatenate([jnp.where(first, rows, other), jnp.where(first, other, rows)], axis=0)
        )
    return found


def other_core(value):
    return lax.ppermute(value, "tensor", [(0, 1), (1, 0), (2, 3), (3, 2)])


def both_halves(half):
    return jnp.concatenate([half, other_core(half)], axis=0)


class Swaps:
    def inputs(self, tokens, targets):
        half, target_half = half_rows(tokens, targets)
        return both_halves(half), target_half

    def residual(self, term, source, targets=None):
        half = source.shape[0] // 2
        theirs = other_core(term(source[half:]))
        chip, sent = by_rows(
            chip_sum_body, "chip_sum", (jnp.float32, jnp.bfloat16), term(source[:half]), theirs
        )
        beyond = lax.ppermute(sent, "tensor", [(0, 2), (2, 0), (1, 3), (3, 1)])
        if targets is None:
            (piece,) = by_rows(tangent_body, "tangent_res", (jnp.bfloat16,), chip, beyond)
        else:
            (piece,) = by_rows(residual_body, "residual", (jnp.bfloat16,), chip, beyond, targets)
        return both_halves(piece)


class Gathers:
    def whole(self, rows):
        return lax.all_gather(rows, "tensor", axis=0, tiled=True)

    def inputs(self, tokens, targets):
        return self.whole(tokens), targets

    def residual(self, term, source, targets=None):
        total = lax.psum_scatter(term(source), "tensor", scatter_dimension=0, tiled=True)
        if targets is not None:
            total = total - targets.astype(jnp.float32)
        return self.whole(total.astype(jnp.bfloat16))


def ring_order(count):
    if count == 8:
        return [0, 2, 4, 6, 7, 5, 3, 1]
    return list(range(count))


def ring_gather(block, axis):
    count = lax.axis_size("replica")
    order = ring_order(count)
    onward = [(order[i], order[(i + 1) % count]) for i in range(count)]
    back = [(b, a) for a, b in onward]
    place = [0] * count
    for at, replica in enumerate(order):
        place[replica] = at
    here = jnp.array(place, jnp.int32)[lax.axis_index("replica")]
    owner = jnp.array(order, jnp.int32)
    extent = block.shape[axis]
    shape = list(block.shape)
    shape[axis] = extent * count
    whole = blank(tuple(shape), block.dtype)

    def put(whole, piece, step, start=0):
        at = owner[jnp.mod(here + step, count)] * extent + start
        index = [0] * block.ndim
        index[axis] = at
        return lax.dynamic_update_slice(whole, piece, index)

    whole = put(whole, block, 0)
    ahead = behind = block
    full_steps = (count - 1) // 2
    near_end = block
    for step in range(1, full_steps + 1):
        ahead = send(ahead, onward)
        behind = send(behind, back)
        if step == full_steps - 1:
            near_end = ahead
        whole = put(whole, ahead, -step)
        whole = put(whole, behind, step)
    if count % 2 == 0:
        half = extent // 2
        first = lax.slice_in_dim(ahead, 0, half, axis=axis)
        second = lax.slice_in_dim(behind, half, extent, axis=axis)
        whole = put(whole, send(first, onward), -(full_steps + 1))
        whole = put(whole, send(second, back), full_steps + 1, half)
    return whole, near_end


def link_matrix(neighbours, numerators):
    count = neighbours.shape[0]
    ids = jnp.arange(count, dtype=neighbours.dtype)
    listed = jnp.sum(
        jnp.where(neighbours[:, :, None] == ids[None, None, :], numerators[:, :, None], 0), axis=1
    )
    own = DEN - jnp.sum(numerators, axis=1)
    return (listed + jnp.diag(own)).astype(jnp.float32) / DEN


class Grid:
    outer = [(2 * a + x, 2 * b + x) for a, b in ((0, 1), (1, 0), (2, 3), (3, 2)) for x in (0, 1)]
    inner = [(2 * a + x, 2 * b + x) for a, b in ((1, 2), (2, 1)) for x in (0, 1)]
    across = [(2 * z + x, 2 * z + 1 - x) for z in range(4) for x in (0, 1)]

    @staticmethod
    def picks():
        found = np.zeros((8, 10, 8, 8), np.float32)
        for r in range(8):
            z, x = divmod(r, 2)
            inside = z in (1, 2)
            swapped = 2 * (z ^ 1) + x
            middle = 2 * (3 - z) + x
            far = (6 if z == 1 else 0) + x
            other = 2 * z + 1 - x
            edge = (0 if z == 1 else 6) + x
            found[r, 0, r, r] = found[r, 1, r, swapped] = 1
            found[r, 4, other, r] = found[r, 5, other, swapped] = 1
            if inside:
                found[r, 2, r, middle] = found[r, 3, r, far] = 1
                found[r, 6, other, middle] = 1
                found[r, 7, edge, middle] = found[r, 8, edge, far] = 1
        found[2, 9, 0, 7] = found[5, 9, 7, 0] = 1
        return found


LAG = 2
STEPS = 2


def tick_kernel(plan, inv_width, *refs):
    names, results = plan
    got = dict(zip(names + results, refs))
    scale_ref = got["scales"]

    def weighted(first, *parts):
        total = None
        for k, part in enumerate(parts):
            term = scale_ref[first + k] * got[part][...].astype(jnp.float32)
            total = term if total is None else total + term
        return total

    put = {}
    if "grads" in got:
        slope = (
            jnp.dot(got["tokens_t"][...], got["grads"][...], preferred_element_type=jnp.float32)
            * inv_width
        )
        base = got["base"][...].astype(jnp.float32)
        tracked = got["tracker"][...].astype(jnp.float32)
        if "step" in names:
            ratio = slope / jnp.maximum(tracked, floor_value)
            made = base - step_size * jnp.clip(ratio, -1.0, 1.0)
        else:
            made = tracker_decay * tracked + (1.0 - tracker_decay) * base * slope
        put["made"] = made.astype(jnp.bfloat16)
    if "cross_own" in got:
        put["cross"] = weighted(4, "cross_own", "cross_swapped", "cross_middle").astype(jnp.bfloat16)
        put["pass_swapped"] = got["cross_swapped"][...]
    if "pass_far" in got:
        put["pass_far"] = got["pass_far"][...]
    if "out_middle" in got:
        put["outward"] = weighted(7, "out_middle", "out_far", "out_wrapped").astype(jnp.bfloat16)
    step = pl.program_id(0)
    for result in results:
        if result != "mixed":
            offset = 0
            for piece in result.split(":")[1].split("+"):
                rows = put[piece].shape[0]
                start = pl.multiple_of(offset + step * rows, rows)
                got[result][pl.ds(start, rows), :] = put[piece]
                offset += rows * STEPS
    if "mixed" in got:
        total = weighted(0, "own", "swapped", "middle", "far")
        total = total + got["sideways"][...].astype(jnp.float32)
        got["mixed"][...] = (total + got["rest"][...].astype(jnp.float32)).astype(jnp.bfloat16)


class Pipeline:
    def __init__(self, links, full_rows, width):
        me = lax.axis_index("replica")
        self.scales = jnp.sum(jnp.asarray(Grid.picks())[me] * links, axis=(1, 2))
        self.full_rows, self.width = full_rows, width
        self.place = {}
        self.last = None

    def parts(self, count):
        unit = self.full_rows // 64
        head, tail = [2, 2], [2, 2, 1, 1, 1, 1]
        found = []
        for which in range(count):
            ends = (head if which == 0 else []), (tail if which == count - 1 else [])
            middle = (64 - sum(ends[0]) - sum(ends[1])) // 4
            row = 0
            for size in ends[0] + [4] * middle + ends[1]:
                found.append((which, row, size * unit))
                row += size * unit
        return found

    def run(self, sources):
        parts = self.parts(len(sources))
        mixed = [None] * len(sources)
        for tick in range(len(parts) + 4 * LAG):
            self.tick(tick, parts, sources, mixed)
        return mixed

    def tick(self, tick, parts, sources, mixed):
        width = self.width
        count = len(parts)
        names, operands, specs = ["scales"], [self.scales], [pl.BlockSpec(memory_space=pltpu.SMEM)]
        place = self.place

        def row_spec(depth, start, rows):
            block = rows // STEPS
            return pl.BlockSpec((block, depth), lambda i: (start // block + i, 0))

        def add(name, key):
            array, start = place[key]
            names.append(name)
            operands.append(array)
            specs.append(row_spec(width, start, parts[key[1]][2]))

        payloads = {"outer": [], "inner": [], "across": []}
        flops = 0
        part = tick - 3 * LAG
        if 0 <= part < count:
            add("out_middle", ("middle", part))
            add("out_far", ("far", part))
            add("out_wrapped", ("wrapped", part))
            payloads["outer"].append(("outward", "rest", part))
        part = tick - 2 * LAG
        if 0 <= part < count:
            add("pass_far", ("far", part))
            payloads["across"].append(("pass_far", "wrapped", part))
        part = tick - LAG
        if 0 <= part < count:
            add("cross_own", ("own", part))
            add("cross_swapped", ("swapped", part))
            add("cross_middle", ("middle", part))
            payloads["inner"].append(("pass_swapped", "far", part))
            payloads["across"].append(("cross", "sideways", part))
        part = tick
        if part < count:
            which, start, rows = parts[part]
            tokens_t, grads, base, tracker, kind = sources[which]
            depth = grads.shape[0]
            names += ["tokens_t", "grads", "base", "tracker", kind]
            operands += [tokens_t, grads, base, tracker, self.scales]
            specs += [
                row_spec(depth, start, rows),
                pl.BlockSpec((depth, width), lambda i: (0, 0)),
                row_spec(width, start, rows),
                row_spec(width, start, rows),
                pl.BlockSpec(memory_space=pltpu.SMEM),
            ]
            payloads["outer"].append(("made", "swapped", part))
            payloads["inner"].append(("made", "middle", part))
            flops += 2 * rows * depth * width
        results, shapes, out_specs = [], [], []
        ways = [way for way, pieces in payloads.items() if pieces]
        moved = 0
        for way in ways:
            rows = sum(parts[piece[2]][2] for piece in payloads[way])
            moved += 2 * rows
            results.append(way + ":" + "+".join(piece[0] for piece in payloads[way]))
            shapes.append(jax.ShapeDtypeStruct((rows, width), jnp.bfloat16))
            out_specs.append(pl.BlockSpec((rows, width), lambda i: (0, 0)))
        aliases = {}
        part = tick - 4 * LAG
        if 0 <= part < count:
            for name in ("own", "swapped", "middle", "far", "sideways", "rest"):
                add(name, (name, part))
            which, start, rows = parts[part]
            if mixed[which] is not None:
                aliases = {len(operands): len(results)}
                names.append("target")
                operands.append(mixed[which])
                specs.append(pl.BlockSpec(memory_space=pl.ANY))
            moved += 7 * rows
            results.append("mixed")
            shapes.append(jax.ShapeDtypeStruct((self.full_rows, width), jnp.bfloat16))
            out_specs.append(row_spec(width, start, rows))
        if self.last is not None:
            names.append("earlier")
            operands.append(self.last)
            specs.append(pl.BlockSpec(memory_space=pl.ANY))
        got = pl.pallas_call(
            functools.partial(
                tick_kernel, (tuple(names), tuple(results)), 1.0 / math.sqrt(self.full_rows)
            ),
            grid=(STEPS,),
            in_specs=specs,
            out_specs=out_specs,
            out_shape=shapes,
            input_output_aliases=aliases,
            compiler_params=pltpu.CompilerParams(vmem_limit_bytes=VMEM_BYTES),
            cost_estimate=pl.CostEstimate(
                flops=flops, bytes_accessed=2 * moved * width, transcendentals=0
            ),
            name="tick",
        )(*operands)
        if results[-1] == "mixed":
            mixed[which] = got[-1]
        for way, payload in zip(ways, got):
            self.last = payload
            received = send(payload, getattr(Grid, way))
            start = 0
            for _, name, part in payloads[way]:
                place[name, part] = (received, start)
                if name == "swapped":
                    place["own", part] = (payload, start)
                start += parts[part][2]


class OffsetMixer:
    offsets = (1, -1, 2, -2, 4, -4)

    def __init__(self, links):
        count = lax.axis_size("replica")
        me = lax.axis_index("replica")
        self.steps = sorted({offset % count for offset in self.offsets})
        columns = jnp.stack([me] + [jnp.mod(me - step, count) for step in self.steps])
        self.scales = links[me][columns]
        self.pairs = [[(s, (s + step) % count) for s in range(count)] for step in self.steps]

    def mix(self, part):
        parts = [part] + [send(part, pairs) for pairs in self.pairs]
        return weighted_sum("mixed_rows", self.scales, parts)


def local(
    tokens, targets, gate_weight, probes, tracker, up_weight, down_weight, neighbours, numerators
):
    weight_now = gate_weight[0]
    tracker_now = tracker[0]
    probe_here = probes[0]
    width = weight_now.shape[0]
    hidden_units = down_weight.shape[0] * lax.axis_size("tensor")
    inv_width = 1.0 / math.sqrt(width)
    inv_hidden = 1.0 / math.sqrt(hidden_units)

    links = link_matrix(neighbours, numerators)

    group = Swaps() if lax.axis_size("tensor") == 4 else Gathers()
    gathered, target_rows = group.inputs(tokens[0], targets[0])
    gathered_t = turned(gathered)
    up_full, near_end = ring_gather(up_weight, 0)
    down_full, _ = ring_gather(after(down_weight, near_end), 1)

    gate_pre = jnp.dot(gathered, weight_now, preferred_element_type=jnp.float32) * inv_width
    probe_pre = jnp.dot(gathered, probe_here, preferred_element_type=jnp.float32) * inv_width
    up_pre = jnp.dot(gathered, up_full, preferred_element_type=jnp.float32) * inv_width
    logistic = jax.nn.sigmoid(gate_pre)
    activated = gate_pre * logistic
    slope_one = logistic * (1.0 + gate_pre * (1.0 - logistic))
    slope_two = logistic * (1.0 - logistic) * (2.0 + gate_pre * (1.0 - 2.0 * logistic))
    hidden = (activated * up_pre).astype(jnp.bfloat16)
    tangent_hidden = (slope_one * probe_pre * up_pre).astype(jnp.bfloat16)

    def forward_term(source):
        return jnp.dot(source, down_full, preferred_element_type=jnp.float32) * inv_hidden

    def backward_rows(piece):
        return (
            lax.dot_general(
                piece, down_full, (((1,), (1,)), ((), ())), preferred_element_type=jnp.float32
            )
            * inv_hidden
        )

    grad_hidden = backward_rows(group.residual(forward_term, hidden, target_rows))
    grad_gate = (grad_hidden * up_pre * slope_one).astype(jnp.bfloat16)

    tangent_grad = backward_rows(group.residual(forward_term, tangent_hidden))
    tangent_gate = (
        (tangent_grad * slope_one + grad_hidden * slope_two * probe_pre) * up_pre
    ).astype(jnp.bfloat16)

    stepping = (gathered_t, grad_gate, weight_now, tracker_now)
    tracking = (gathered_t, tangent_gate, probe_here, tracker_now)
    if lax.axis_size("replica") == 8:
        pipeline = Pipeline(links, width, weight_now.shape[1])
        mixed_weights, mixed_tracker = pipeline.run([(*stepping, "step"), (*tracking, "track")])
    else:
        mixer = OffsetMixer(links)
        mixed_weights = mixer.mix(update_rows(step_body, "stepped_rows", *stepping))
        mixed_tracker = mixer.mix(update_rows(track_body, "tracked_rows", *tracking))
    return (mixed_weights[None], mixed_tracker[None])


def solution(mesh):
    return jax.shard_map(
        local,
        mesh=mesh,
        in_specs=(
            P("replica", "tensor", None),
            P("replica", "tensor", None),
            P("replica", None, "tensor"),
            P("replica", None, "tensor"),
            P("replica", None, "tensor"),
            P("replica", "tensor"),
            P("tensor", "replica"),
            P(),
            P(),
        ),
        out_specs=(P("replica", None, "tensor"), P("replica", None, "tensor")),
        check_vma=False,
    )
```

```python
import functools
import math

import jax
import jax.numpy as jnp
import numpy as np
from jax import lax
from jax.experimental import pallas as pl
from jax.experimental.pallas import tpu as pltpu
from jax.sharding import PartitionSpec as P

DEN = 64

step_size = 0.1
floor_value = 0.1
tracker_decay = 0.75

VMEM_BYTES = 16 * 1024 * 1024
TICK_VMEM_BYTES = 40 * 1024 * 1024


def send(value, pairs):
    return lax.ppermute(value, "replica", pairs)


def step_body(inv_width, xt_ref, grad_ref, weight_ref, tracker_ref, out_ref):
    gradient = jnp.dot(xt_ref[...], grad_ref[...], preferred_element_type=jnp.float32) * inv_width
    ratio = gradient / jnp.maximum(tracker_ref[...].astype(jnp.float32), floor_value)
    out_ref[...] = (
        weight_ref[...].astype(jnp.float32) - step_size * jnp.clip(ratio, -1.0, 1.0)
    ).astype(out_ref.dtype)


def track_body(inv_width, xt_ref, grad_ref, probe_ref, tracker_ref, out_ref):
    curvature = jnp.dot(xt_ref[...], grad_ref[...], preferred_element_type=jnp.float32) * inv_width
    out_ref[...] = (
        tracker_decay * tracker_ref[...].astype(jnp.float32)
        + (1.0 - tracker_decay) * probe_ref[...].astype(jnp.float32) * curvature
    ).astype(out_ref.dtype)


def update_rows(body, name, tokens_t, grads, first, second):
    rows, width = first.shape
    depth = grads.shape[0]
    size = min(rows, 256)
    row_spec = pl.BlockSpec((size, width), lambda i: (i, 0))
    return pl.pallas_call(
        functools.partial(body, 1.0 / math.sqrt(rows)),
        grid=(rows // size,),
        in_specs=[
            pl.BlockSpec((size, depth), lambda i: (i, 0)),
            pl.BlockSpec((depth, width), lambda i: (0, 0)),
            row_spec,
            row_spec,
        ],
        out_specs=row_spec,
        out_shape=jax.ShapeDtypeStruct((rows, width), jnp.bfloat16),
        compiler_params=pltpu.CompilerParams(vmem_limit_bytes=VMEM_BYTES),
        name=name,
    )(tokens_t, grads, first, second)


def weighted_body(count, scale_ref, *refs):
    total = scale_ref[0] * refs[0][...].astype(jnp.float32)
    for k in range(1, count):
        total = total + scale_ref[k] * refs[k][...].astype(jnp.float32)
    refs[-1][...] = total.astype(refs[-1].dtype)


def weighted_sum(name, scales, parts):
    rows, width = parts[0].shape
    size = min(rows, 128)
    row_spec = pl.BlockSpec((size, width), lambda i: (i, 0))
    return pl.pallas_call(
        functools.partial(weighted_body, len(parts)),
        grid=(rows // size,),
        in_specs=[pl.BlockSpec(memory_space=pltpu.SMEM)] + [row_spec] * len(parts),
        out_specs=row_spec,
        out_shape=jax.ShapeDtypeStruct((rows, width), jnp.bfloat16),
        compiler_params=pltpu.CompilerParams(vmem_limit_bytes=VMEM_BYTES),
        name=name,
    )(scales, *parts)


def after(value, *earlier):
    def body(value_ref, *refs):
        refs[-1][...] = value_ref[...]

    return pl.pallas_call(
        body,
        in_specs=[pl.BlockSpec(memory_space=pltpu.VMEM)]
        + [pl.BlockSpec(memory_space=pl.ANY)] * len(earlier),
        out_specs=pl.BlockSpec(memory_space=pltpu.VMEM),
        out_shape=jax.ShapeDtypeStruct(value.shape, value.dtype),
        compiler_params=pltpu.CompilerParams(vmem_limit_bytes=VMEM_BYTES),
        name="after",
    )(value, *earlier)


def blank(shape, dtype):
    def body(out_ref):
        pass

    return pl.pallas_call(
        body,
        out_specs=pl.BlockSpec(memory_space=pl.ANY),
        out_shape=jax.ShapeDtypeStruct(shape, dtype),
        name="blank",
    )()


def by_rows(body, name, results, *operands, earlier=()):
    count = len(operands)

    def without_earlier(*refs):
        body(*refs[:count], *refs[count + len(earlier) :])

    rows, width = operands[0].shape
    size = rows // 4 if rows % 64 == 0 else rows
    row_spec = pl.BlockSpec((size, width), lambda i: (i, 0))
    return pl.pallas_call(
        without_earlier,
        grid=(rows // size,),
        in_specs=[row_spec] * count + [pl.BlockSpec(memory_space=pl.ANY)] * len(earlier),
        out_specs=[row_spec] * len(results),
        out_shape=[jax.ShapeDtypeStruct((rows, width), kind) for kind in results],
        compiler_params=pltpu.CompilerParams(vmem_limit_bytes=VMEM_BYTES),
        name=name,
    )(*operands, *earlier)


def chip_sum_body(mine_ref, theirs_ref, sum_ref, sent_ref):
    total = mine_ref[...] + theirs_ref[...]
    sum_ref[...] = total
    sent_ref[...] = total.astype(sent_ref.dtype)


def residual_body(chip_ref, beyond_ref, target_ref, out_ref):
    total = chip_ref[...] + beyond_ref[...].astype(jnp.float32)
    out_ref[...] = (total - target_ref[...].astype(jnp.float32)).astype(out_ref.dtype)


def tangent_body(chip_ref, beyond_ref, out_ref):
    total = chip_ref[...] + beyond_ref[...].astype(jnp.float32)
    out_ref[...] = total.astype(out_ref.dtype)


def backward_product(inv_hidden, res_ref, down_ref):
    return (
        lax.dot_general(
            res_ref[...],
            down_ref[...],
            (((1,), (1,)), ((), ())),
            preferred_element_type=jnp.float32,
        )
        * inv_hidden
    )


def gate_body(inv_hidden, res_ref, down_ref, factor_ref, hidden_ref, gate_ref):
    grad = backward_product(inv_hidden, res_ref, down_ref)
    hidden_ref[...] = grad
    gate_ref[...] = (grad * factor_ref[...]).astype(gate_ref.dtype)


def tangent_gate_body(inv_hidden, res_ref, down_ref, factor_ref, hidden_ref, curve_ref, gate_ref):
    grad = backward_product(inv_hidden, res_ref, down_ref)
    gate = grad * factor_ref[...] + hidden_ref[...] * curve_ref[...]
    gate_ref[...] = gate.astype(gate_ref.dtype)


def backward(body, name, inv_hidden, kinds, res, down, *factors):
    rows, width = res.shape
    units = down.shape[0]
    size = 256 if units % 256 == 0 else units
    unit_spec = pl.BlockSpec((rows, size), lambda i: (0, i))
    return pl.pallas_call(
        functools.partial(body, inv_hidden),
        grid=(units // size,),
        in_specs=[
            pl.BlockSpec((rows, width), lambda i: (0, 0)),
            pl.BlockSpec((size, width), lambda i: (i, 0)),
        ]
        + [unit_spec] * len(factors),
        out_specs=[unit_spec] * len(kinds),
        out_shape=[jax.ShapeDtypeStruct((rows, units), kind) for kind in kinds],
        compiler_params=pltpu.CompilerParams(vmem_limit_bytes=VMEM_BYTES),
        cost_estimate=pl.CostEstimate(
            flops=2 * rows * width * units,
            bytes_accessed=2 * units * width + 10 * rows * units,
            transcendentals=0,
        ),
        name=name,
    )(res, down, *factors)


def turned(value):
    rows, width = value.shape
    size = 256

    def body(value_ref, out_ref):
        out_ref[...] = value_ref[...].T

    return pl.pallas_call(
        body,
        grid=(width // size,),
        in_specs=[pl.BlockSpec((rows, size), lambda i: (0, i))],
        out_specs=pl.BlockSpec((size, rows), lambda i: (i, 0)),
        out_shape=jax.ShapeDtypeStruct((width, rows), value.dtype),
        compiler_params=pltpu.CompilerParams(vmem_limit_bytes=VMEM_BYTES),
        name="turned",
    )(value)


def half_rows(rows):
    beyond = lax.ppermute(rows, "tensor", [(0, 2), (2, 0), (1, 3), (3, 1)])
    first = lax.axis_index("tensor") < 2
    return jnp.concatenate(
        [jnp.where(first, rows, beyond), jnp.where(first, beyond, rows)], axis=0
    )


def other_core(value):
    return lax.ppermute(value, "tensor", [(0, 1), (1, 0), (2, 3), (3, 2)])


def both_halves(half):
    return jnp.concatenate([half, other_core(half)], axis=0)


class Swaps:
    def inputs(self, tokens, targets):
        return both_halves(half_rows(tokens)), half_rows(targets)

    def terms(self, term, source):
        half = source.shape[0] // 2
        theirs = other_core(term(source[half:]))
        return term(source[:half]), theirs

    def sums(self, terms, earlier=()):
        chip, sent = by_rows(
            chip_sum_body, "chip_sum", (jnp.float32, jnp.bfloat16), *terms, earlier=earlier
        )
        return chip, lax.ppermute(sent, "tensor", [(0, 2), (2, 0), (1, 3), (3, 1)])

    def residuals(self, term, hidden, tangent_hidden, targets, earlier):
        sums = self.sums(self.terms(term, hidden), earlier)
        tangent_terms = self.terms(term, tangent_hidden)
        (piece,) = by_rows(
            residual_body, "residual", (jnp.bfloat16,), *sums, targets, earlier=tangent_terms
        )
        tangent_sums = self.sums(tangent_terms, (piece,))

        def tangent(*earlier):
            (tangent_piece,) = by_rows(
                tangent_body, "tangent_res", (jnp.bfloat16,), *tangent_sums, earlier=earlier
            )
            return tangent_piece, both_halves(tangent_piece)

        return both_halves(piece), tangent


class Gathers:
    def whole(self, rows):
        return lax.all_gather(rows, "tensor", axis=0, tiled=True)

    def inputs(self, tokens, targets):
        return self.whole(tokens), targets

    def residuals(self, term, hidden, tangent_hidden, targets, earlier):
        first, second = (
            lax.psum_scatter(term(source), "tensor", scatter_dimension=0, tiled=True)
            for source in (hidden, tangent_hidden)
        )
        residual = (first - targets.astype(jnp.float32)).astype(jnp.bfloat16)
        tangent_piece = second.astype(jnp.bfloat16)
        return self.whole(residual), lambda *earlier: (tangent_piece, self.whole(tangent_piece))


def ring_order(count):
    if count == 8:
        return [0, 2, 4, 6, 7, 5, 3, 1]
    return list(range(count))


def ring_gather(block, axis):
    count = lax.axis_size("replica")
    order = ring_order(count)
    onward = [(order[i], order[(i + 1) % count]) for i in range(count)]
    back = [(b, a) for a, b in onward]
    place = [0] * count
    for at, replica in enumerate(order):
        place[replica] = at
    here = jnp.array(place, jnp.int32)[lax.axis_index("replica")]
    owner = jnp.array(order, jnp.int32)
    extent = block.shape[axis]
    shape = list(block.shape)
    shape[axis] = extent * count
    whole = blank(tuple(shape), block.dtype)

    def put(whole, piece, step, start=0):
        at = owner[jnp.mod(here + step, count)] * extent + start
        index = [0] * block.ndim
        index[axis] = at
        return lax.dynamic_update_slice(whole, piece, index)

    whole = put(whole, block, 0)
    ahead = behind = block
    full_steps = (count - 1) // 2
    first_block = block
    for step in range(1, full_steps + 1):
        ahead = send(ahead, onward)
        behind = send(behind, back)
        if step == 1:
            first_block = ahead
        whole = put(whole, ahead, -step)
        whole = put(whole, behind, step)
    if count % 2 == 0:
        half = extent // 2
        first = lax.slice_in_dim(ahead, 0, half, axis=axis)
        second = lax.slice_in_dim(behind, half, extent, axis=axis)
        whole = put(whole, send(first, onward), -(full_steps + 1))
        whole = put(whole, send(second, back), full_steps + 1, half)
    return whole, first_block


def link_matrix(neighbours, numerators):
    count = neighbours.shape[0]
    ids = jnp.arange(count, dtype=neighbours.dtype)
    listed = jnp.sum(
        jnp.where(neighbours[:, :, None] == ids[None, None, :], numerators[:, :, None], 0), axis=1
    )
    own = DEN - jnp.sum(numerators, axis=1)
    return (listed + jnp.diag(own)).astype(jnp.float32) / DEN


class Grid:
    outer = [(2 * a + x, 2 * b + x) for a, b in ((0, 1), (1, 0), (2, 3), (3, 2)) for x in (0, 1)]
    inner = [(2 * a + x, 2 * b + x) for a, b in ((1, 2), (2, 1)) for x in (0, 1)]
    across = [(2 * z + x, 2 * z + 1 - x) for z in range(4) for x in (0, 1)]

    @staticmethod
    def picks():
        found = np.zeros((8, 10, 8, 8), np.float32)
        for r in range(8):
            z, x = divmod(r, 2)
            inside = z in (1, 2)
            swapped = 2 * (z ^ 1) + x
            middle = 2 * (3 - z) + x
            far = (6 if z == 1 else 0) + x
            other = 2 * z + 1 - x
            edge = (0 if z == 1 else 6) + x
            found[r, 0, r, r] = found[r, 1, r, swapped] = 1
            found[r, 4, other, r] = found[r, 5, other, swapped] = 1
            if inside:
                found[r, 2, r, middle] = found[r, 3, r, far] = 1
                found[r, 6, other, middle] = 1
                found[r, 7, edge, middle] = found[r, 8, edge, far] = 1
        found[2, 9, 0, 7] = found[5, 9, 7, 0] = 1
        return found


STEPS = 2


def tick_kernel(plan, inv_width, *refs):
    names, results = plan
    got = dict(zip(names + results, refs))
    scale_ref = got["scales"]

    def weighted(first, *parts):
        total = None
        for k, part in enumerate(parts):
            term = scale_ref[first + k] * got[part][...].astype(jnp.float32)
            total = term if total is None else total + term
        return total

    put = {}
    if "grads" in got:
        slope = (
            jnp.dot(got["tokens_t"][...], got["grads"][...], preferred_element_type=jnp.float32)
            * inv_width
        )
        base = got["base"][...].astype(jnp.float32)
        tracked = got["tracker"][...].astype(jnp.float32)
        if "step" in names:
            ratio = slope / jnp.maximum(tracked, floor_value)
            made = base - step_size * jnp.clip(ratio, -1.0, 1.0)
        else:
            made = tracker_decay * tracked + (1.0 - tracker_decay) * base * slope
        put["made"] = made.astype(jnp.bfloat16)
    if "cross_own" in got:
        put["cross"] = weighted(4, "cross_own", "cross_swapped", "cross_middle").astype(jnp.bfloat16)
    if "pass_swapped" in got:
        put["pass_swapped"] = got["pass_swapped"][...]
    if "pass_far" in got:
        put["pass_far"] = got["pass_far"][...]
    if "out_middle" in got:
        put["outward"] = weighted(7, "out_middle", "out_far", "out_wrapped").astype(jnp.bfloat16)
    step = pl.program_id(0)
    for result in results:
        if result != "mixed":
            offset = 0
            for at, piece in enumerate(result.split(":")[1].split("+")):
                if len(got[result].shape) == 3:
                    got[result][at] = put[piece]
                    continue
                rows = put[piece].shape[0]
                start = pl.multiple_of(offset + step * rows, rows)
                got[result][pl.ds(start, rows), :] = put[piece]
                offset += rows * STEPS
    if "mixed" in got:
        total = weighted(0, "own", "swapped", "middle", "far")
        total = total + got["sideways"][...].astype(jnp.float32)
        got["mixed"][...] = (total + got["rest"][...].astype(jnp.float32)).astype(jnp.bfloat16)


class Pipeline:
    def __init__(self, scales, full_rows, width):
        self.scales = scales
        self.full_rows, self.width = full_rows, width
        self.place = {}
        self.received = {}
        self.last = None

    def parts(self, count):
        unit = self.full_rows // 64
        sizes = [[4] * 16 for _ in range(count)]
        sizes[0] = [2] * 4 + [4] * 14
        sizes[-1] = [4] * 15 + [2] * 2
        found = []
        for which, units in enumerate(sizes):
            row = 0
            for size in units:
                found.append((which, row, size * unit))
                row += size * unit
        return found

    def run(self, stepping, tracking):
        self.sources = [(*stepping, "step"), None]
        self.before = {}
        self.order = self.parts(2)
        self.mixed = [None, None]
        for tick in range(len(self.order) + 7):
            if tick == 3:
                tracked, (first, second) = tracking(self.last)
                self.sources[1] = (*tracked, "track")
                self.before = {6: [first], 9: [second]}
            self.kernel(("outer", "inner"), tick)
            self.kernel(("across",), tick)
        return self.mixed

    def kernel(self, ways, tick):
        width, parts, place, mixed = self.width, self.order, self.place, self.mixed
        count = len(parts)
        names, operands, specs = ["scales"], [self.scales], [pl.BlockSpec(memory_space=pltpu.SMEM)]

        def row_spec(depth, start, rows):
            block = rows // STEPS
            assert start % block == 0
            return pl.BlockSpec((block, depth), lambda i: (start // block + i, 0))

        def add(name, key):
            array, start = place[key]
            rows = parts[key[1]][2]
            names.append(name)
            operands.append(array)
            if array.ndim == 3:
                item = start // rows
                specs.append(pl.BlockSpec((None, rows // STEPS, width), lambda i: (item, i, 0)))
            else:
                specs.append(row_spec(width, start, rows))

        def add_earlier(array):
            names.append("earlier")
            operands.append(array)
            specs.append(pl.BlockSpec(memory_space=pl.ANY))

        payloads = {way: [] for way in ways}
        flops = moved = 0
        if "inner" in ways:
            part = tick
            if part < count:
                which, start, rows = parts[part]
                tokens_t, grads, base, tracker, kind = self.sources[which]
                depth = grads.shape[0]
                names += ["tokens_t", "grads", "base", "tracker", kind]
                operands += [tokens_t, grads, base, tracker, self.scales]
                specs += [
                    row_spec(depth, start, rows),
                    pl.BlockSpec((depth, width), lambda i: (0, 0)),
                    row_spec(width, start, rows),
                    row_spec(width, start, rows),
                    pl.BlockSpec(memory_space=pltpu.SMEM),
                ]
                payloads["outer"].append(("made", "swapped", part))
                payloads["inner"].append(("made", "middle", part))
                flops += 2 * rows * depth * width
                moved += 2 * rows
            part = tick - 2
            if 0 <= part < count:
                add("pass_swapped", ("swapped", part))
                payloads["inner"].append(("pass_swapped", "far", part))
            part = tick - 5
            if 0 <= part < count:
                add("out_middle", ("middle", part))
                add("out_far", ("far", part))
                add("out_wrapped", ("wrapped", part))
                payloads["outer"].append(("outward", "rest", part))
                moved += 2 * parts[part][2]
            for array in self.before.get(tick, ()):
                add_earlier(array)
        else:
            part = tick - 2
            if 0 <= part < count:
                add("cross_own", ("own", part))
                add("cross_swapped", ("swapped", part))
                add("cross_middle", ("middle", part))
                payloads["across"].append(("cross", "sideways", part))
                moved += 2 * parts[part][2]
            part = tick - 3
            if 0 <= part < count:
                add("pass_far", ("far", part))
                payloads["across"].append(("pass_far", "wrapped", part))
            if ("inner", tick - 1) in self.received:
                add_earlier(self.received["inner", tick - 1])
        results, shapes, out_specs = [], [], []
        ways = [way for way, pieces in payloads.items() if pieces]
        for way in ways:
            payloads[way].sort(key=lambda piece: -parts[piece[2]][2])
            rows = sum(parts[piece[2]][2] for piece in payloads[way])
            moved += 2 * rows
            results.append(way + ":" + "+".join(piece[0] for piece in payloads[way]))
            sizes = {parts[piece[2]][2] for piece in payloads[way]}
            if len(sizes) == 1:
                items, each = len(payloads[way]), sizes.pop()
                shapes.append(jax.ShapeDtypeStruct((items, each, width), jnp.bfloat16))
                out_specs.append(pl.BlockSpec((items, each // STEPS, width), lambda i: (0, i, 0)))
            else:
                shapes.append(jax.ShapeDtypeStruct((rows, width), jnp.bfloat16))
                out_specs.append(pl.BlockSpec((rows, width), lambda i: (0, 0)))
        aliases = {}
        part = tick - 7
        mixing = 0 <= part < count and "inner" not in payloads
        if mixing:
            for name in ("own", "swapped", "middle", "far", "sideways", "rest"):
                add(name, (name, part))
            which, start, rows = parts[part]
            if mixed[which] is not None:
                aliases = {len(operands): len(results)}
                names.append("target")
                operands.append(mixed[which])
                specs.append(pl.BlockSpec(memory_space=pl.ANY))
            moved += 7 * rows
            results.append("mixed")
            shapes.append(jax.ShapeDtypeStruct((self.full_rows, width), jnp.bfloat16))
            out_specs.append(row_spec(width, start, rows))
        if not results:
            return
        if self.last is not None:
            add_earlier(self.last)
        got = pl.pallas_call(
            functools.partial(
                tick_kernel, (tuple(names), tuple(results)), 1.0 / math.sqrt(self.full_rows)
            ),
            grid=(STEPS,),
            in_specs=specs,
            out_specs=out_specs,
            out_shape=shapes,
            input_output_aliases=aliases,
            compiler_params=pltpu.CompilerParams(vmem_limit_bytes=TICK_VMEM_BYTES),
            cost_estimate=pl.CostEstimate(
                flops=flops, bytes_accessed=2 * moved * width, transcendentals=0
            ),
            name="tick_across" if mixing or "across" in ways else "tick",
        )(*operands)
        if mixing:
            mixed[which] = got[-1]
        for way, payload in zip(ways, got):
            self.last = payload
            received = send(payload, getattr(Grid, way))
            self.received[way, tick] = received
            start = 0
            for _, name, part in payloads[way]:
                place[name, part] = (received, start)
                if name == "swapped":
                    place["own", part] = (payload, start)
                start += parts[part][2]


class OffsetMixer:
    offsets = (1, -1, 2, -2, 4, -4)

    def __init__(self, links):
        count = lax.axis_size("replica")
        me = lax.axis_index("replica")
        self.steps = sorted({offset % count for offset in self.offsets})
        columns = jnp.stack([me] + [jnp.mod(me - step, count) for step in self.steps])
        self.scales = links[me][columns]
        self.pairs = [[(s, (s + step) % count) for s in range(count)] for step in self.steps]

    def mix(self, part):
        parts = [part] + [send(part, pairs) for pairs in self.pairs]
        return weighted_sum("mixed_rows", self.scales, parts)


def local(
    tokens, targets, gate_weight, probes, tracker, up_weight, down_weight, neighbours, numerators
):
    weight_now = gate_weight[0]
    tracker_now = tracker[0]
    probe_here = probes[0]
    width = weight_now.shape[0]
    hidden_units = down_weight.shape[0] * lax.axis_size("tensor")
    inv_width = 1.0 / math.sqrt(width)
    inv_hidden = 1.0 / math.sqrt(hidden_units)

    links = link_matrix(neighbours, numerators)

    group = Swaps() if lax.axis_size("tensor") == 4 else Gathers()
    gathered, target_rows = group.inputs(tokens[0], targets[0])
    gathered_t = turned(gathered)
    scales = jnp.zeros(1)
    if lax.axis_size("replica") == 8:
        scales = jnp.sum(
            jnp.asarray(Grid.picks())[lax.axis_index("replica")] * links, axis=(1, 2)
        )
    up_full, first_block = ring_gather(up_weight, 0)
    down_full, _ = ring_gather(after(down_weight, first_block, target_rows, gathered_t, scales), 1)

    gate_pre = jnp.dot(gathered, weight_now, preferred_element_type=jnp.float32) * inv_width
    probe_pre = jnp.dot(gathered, probe_here, preferred_element_type=jnp.float32) * inv_width
    up_pre = jnp.dot(gathered, up_full, preferred_element_type=jnp.float32) * inv_width
    logistic = jax.nn.sigmoid(gate_pre)
    activated = gate_pre * logistic
    slope_one = logistic * (1.0 + gate_pre * (1.0 - logistic))
    slope_two = logistic * (1.0 - logistic) * (2.0 + gate_pre * (1.0 - 2.0 * logistic))
    hidden = (activated * up_pre).astype(jnp.bfloat16)
    gate_factor = up_pre * slope_one
    curve_factor = slope_two * probe_pre * up_pre
    tangent_hidden = (slope_one * probe_pre * up_pre).astype(jnp.bfloat16)

    def forward_term(source):
        return jnp.dot(source, down_full, preferred_element_type=jnp.float32) * inv_hidden

    residual, tangent_sums = group.residuals(
        forward_term, hidden, tangent_hidden, target_rows, (gate_factor, curve_factor)
    )
    grad_hidden, grad_gate = backward(
        gate_body,
        "backward_gate",
        inv_hidden,
        (jnp.float32, jnp.bfloat16),
        residual,
        down_full,
        gate_factor,
    )

    def tracking(*earlier):
        tangent_piece, tangent_res = tangent_sums(*earlier)
        (tangent_gate,) = backward(
            tangent_gate_body,
            "tangent_gate",
            inv_hidden,
            (jnp.bfloat16,),
            tangent_res,
            down_full,
            gate_factor,
            grad_hidden,
            curve_factor,
        )
        return (gathered_t, tangent_gate, probe_here, tracker_now), (tangent_piece, tangent_gate)

    stepping = (gathered_t, grad_gate, weight_now, tracker_now)
    if lax.axis_size("replica") == 8:
        pipeline = Pipeline(scales, width, weight_now.shape[1])
        mixed_weights, mixed_tracker = pipeline.run(stepping, tracking)
    else:
        mixer = OffsetMixer(links)
        mixed_weights = mixer.mix(update_rows(step_body, "stepped_rows", *stepping))
        mixed_tracker = mixer.mix(update_rows(track_body, "tracked_rows", *tracking()[0]))
    return (mixed_weights[None], mixed_tracker[None])


def solution(mesh):
    return jax.shard_map(
        local,
        mesh=mesh,
        in_specs=(
            P("replica", "tensor", None),
            P("replica", "tensor", None),
            P("replica", None, "tensor"),
            P("replica", None, "tensor"),
            P("replica", None, "tensor"),
            P("replica", "tensor"),
            P("tensor", "replica"),
            P(),
            P(),
        ),
        out_specs=(P("replica", None, "tensor"), P("replica", None, "tensor")),
        check_vma=False,
    )
```

```python
import functools
import math

import jax
import jax.numpy as jnp
import numpy as np
from jax import lax
from jax.experimental import pallas as pl
from jax.experimental.pallas import tpu as pltpu
from jax.sharding import PartitionSpec as P

DEN = 64

step_size = 0.1
floor_value = 0.1
tracker_decay = 0.75

VMEM_BYTES = 16 * 1024 * 1024
TICK_VMEM_BYTES = 40 * 1024 * 1024


def send(value, pairs):
    return lax.ppermute(value, "replica", pairs)


def step_body(inv_width, xt_ref, grad_ref, weight_ref, tracker_ref, out_ref):
    gradient = jnp.dot(xt_ref[...], grad_ref[...], preferred_element_type=jnp.float32) * inv_width
    ratio = gradient / jnp.maximum(tracker_ref[...].astype(jnp.float32), floor_value)
    out_ref[...] = (
        weight_ref[...].astype(jnp.float32) - step_size * jnp.clip(ratio, -1.0, 1.0)
    ).astype(out_ref.dtype)


def track_body(inv_width, xt_ref, grad_ref, probe_ref, tracker_ref, out_ref):
    curvature = jnp.dot(xt_ref[...], grad_ref[...], preferred_element_type=jnp.float32) * inv_width
    out_ref[...] = (
        tracker_decay * tracker_ref[...].astype(jnp.float32)
        + (1.0 - tracker_decay) * probe_ref[...].astype(jnp.float32) * curvature
    ).astype(out_ref.dtype)


def update_rows(body, name, tokens_t, grads, first, second):
    rows, width = first.shape
    depth = grads.shape[0]
    size = min(rows, 256)
    row_spec = pl.BlockSpec((size, width), lambda i: (i, 0))
    return pl.pallas_call(
        functools.partial(body, 1.0 / math.sqrt(rows)),
        grid=(rows // size,),
        in_specs=[
            pl.BlockSpec((size, depth), lambda i: (i, 0)),
            pl.BlockSpec((depth, width), lambda i: (0, 0)),
            row_spec,
            row_spec,
        ],
        out_specs=row_spec,
        out_shape=jax.ShapeDtypeStruct((rows, width), jnp.bfloat16),
        compiler_params=pltpu.CompilerParams(vmem_limit_bytes=VMEM_BYTES),
        name=name,
    )(tokens_t, grads, first, second)


def weighted_body(count, scale_ref, *refs):
    total = scale_ref[0] * refs[0][...].astype(jnp.float32)
    for k in range(1, count):
        total = total + scale_ref[k] * refs[k][...].astype(jnp.float32)
    refs[-1][...] = total.astype(refs[-1].dtype)


def weighted_sum(name, scales, parts):
    rows, width = parts[0].shape
    size = min(rows, 128)
    row_spec = pl.BlockSpec((size, width), lambda i: (i, 0))
    return pl.pallas_call(
        functools.partial(weighted_body, len(parts)),
        grid=(rows // size,),
        in_specs=[pl.BlockSpec(memory_space=pltpu.SMEM)] + [row_spec] * len(parts),
        out_specs=row_spec,
        out_shape=jax.ShapeDtypeStruct((rows, width), jnp.bfloat16),
        compiler_params=pltpu.CompilerParams(vmem_limit_bytes=VMEM_BYTES),
        name=name,
    )(scales, *parts)


def after(value, *earlier):
    def body(value_ref, *refs):
        refs[-1][...] = value_ref[...]

    return pl.pallas_call(
        body,
        in_specs=[pl.BlockSpec(memory_space=pltpu.VMEM)]
        + [pl.BlockSpec(memory_space=pl.ANY)] * len(earlier),
        out_specs=pl.BlockSpec(memory_space=pltpu.VMEM),
        out_shape=jax.ShapeDtypeStruct(value.shape, value.dtype),
        compiler_params=pltpu.CompilerParams(vmem_limit_bytes=VMEM_BYTES),
        name="after",
    )(value, *earlier)


def blank(shape, dtype):
    def body(out_ref):
        pass

    return pl.pallas_call(
        body,
        out_specs=pl.BlockSpec(memory_space=pl.ANY),
        out_shape=jax.ShapeDtypeStruct(shape, dtype),
        name="blank",
    )()


def by_rows(body, name, results, *operands, earlier=()):
    count = len(operands)

    def without_earlier(*refs):
        body(*refs[:count], *refs[count + len(earlier) :])

    rows, width = operands[0].shape
    size = rows // 4 if rows % 64 == 0 else rows
    row_spec = pl.BlockSpec((size, width), lambda i: (i, 0))
    return pl.pallas_call(
        without_earlier,
        grid=(rows // size,),
        in_specs=[row_spec] * count + [pl.BlockSpec(memory_space=pl.ANY)] * len(earlier),
        out_specs=[row_spec] * len(results),
        out_shape=[jax.ShapeDtypeStruct((rows, width), kind) for kind in results],
        compiler_params=pltpu.CompilerParams(vmem_limit_bytes=VMEM_BYTES),
        name=name,
    )(*operands, *earlier)


def chip_sum_body(mine_ref, theirs_ref, sum_ref, sent_ref):
    total = mine_ref[...] + theirs_ref[...]
    sum_ref[...] = total
    sent_ref[...] = total.astype(sent_ref.dtype)


def residual_body(chip_ref, beyond_ref, target_ref, out_ref):
    total = chip_ref[...] + beyond_ref[...].astype(jnp.float32)
    out_ref[...] = (total - target_ref[...].astype(jnp.float32)).astype(out_ref.dtype)


def tangent_body(chip_ref, beyond_ref, out_ref):
    total = chip_ref[...] + beyond_ref[...].astype(jnp.float32)
    out_ref[...] = total.astype(out_ref.dtype)


def backward_product(inv_hidden, res_ref, down_ref):
    return (
        lax.dot_general(
            res_ref[...],
            down_ref[...],
            (((1,), (1,)), ((), ())),
            preferred_element_type=jnp.float32,
        )
        * inv_hidden
    )


def gate_body(inv_hidden, res_ref, down_ref, factor_ref, hidden_ref, gate_ref):
    grad = backward_product(inv_hidden, res_ref, down_ref)
    hidden_ref[...] = grad
    gate_ref[...] = (grad * factor_ref[...]).astype(gate_ref.dtype)


def tangent_gate_body(inv_hidden, res_ref, down_ref, factor_ref, hidden_ref, curve_ref, gate_ref):
    grad = backward_product(inv_hidden, res_ref, down_ref)
    gate = grad * factor_ref[...] + hidden_ref[...] * curve_ref[...]
    gate_ref[...] = gate.astype(gate_ref.dtype)


def backward(body, name, inv_hidden, kinds, res, down, *factors):
    rows, width = res.shape
    units = down.shape[0]
    size = 256 if units % 256 == 0 else units
    unit_spec = pl.BlockSpec((rows, size), lambda i: (0, i))
    return pl.pallas_call(
        functools.partial(body, inv_hidden),
        grid=(units // size,),
        in_specs=[
            pl.BlockSpec((rows, width), lambda i: (0, 0)),
            pl.BlockSpec((size, width), lambda i: (i, 0)),
        ]
        + [unit_spec] * len(factors),
        out_specs=[unit_spec] * len(kinds),
        out_shape=[jax.ShapeDtypeStruct((rows, units), kind) for kind in kinds],
        compiler_params=pltpu.CompilerParams(vmem_limit_bytes=VMEM_BYTES),
        cost_estimate=pl.CostEstimate(
            flops=2 * rows * width * units,
            bytes_accessed=2 * units * width + 10 * rows * units,
            transcendentals=0,
        ),
        name=name,
    )(res, down, *factors)


def turned(value):
    rows, width = value.shape
    size = 256

    def body(value_ref, out_ref):
        out_ref[...] = value_ref[...].T

    return pl.pallas_call(
        body,
        grid=(width // size,),
        in_specs=[pl.BlockSpec((rows, size), lambda i: (0, i))],
        out_specs=pl.BlockSpec((size, rows), lambda i: (i, 0)),
        out_shape=jax.ShapeDtypeStruct((width, rows), value.dtype),
        compiler_params=pltpu.CompilerParams(vmem_limit_bytes=VMEM_BYTES),
        name="turned",
    )(value)


def half_rows(rows):
    beyond = lax.ppermute(rows, "tensor", [(0, 2), (2, 0), (1, 3), (3, 1)])
    first = lax.axis_index("tensor") < 2
    return jnp.concatenate(
        [jnp.where(first, rows, beyond), jnp.where(first, beyond, rows)], axis=0
    )


def other_core(value):
    return lax.ppermute(value, "tensor", [(0, 1), (1, 0), (2, 3), (3, 2)])


def both_halves(half):
    return jnp.concatenate([half, other_core(half)], axis=0)


class Swaps:
    def inputs(self, tokens, targets):
        return both_halves(half_rows(tokens)), half_rows(targets)

    def terms(self, term, source):
        half = source.shape[0] // 2
        theirs = other_core(term(source[half:]))
        return term(source[:half]), theirs

    def sums(self, terms, earlier=()):
        chip, sent = by_rows(
            chip_sum_body, "chip_sum", (jnp.float32, jnp.bfloat16), *terms, earlier=earlier
        )
        return chip, lax.ppermute(sent, "tensor", [(0, 2), (2, 0), (1, 3), (3, 1)])

    def residuals(self, term, hidden, tangent_hidden, targets, earlier):
        sums = self.sums(self.terms(term, hidden), earlier)
        tangent_terms = self.terms(term, tangent_hidden)
        (piece,) = by_rows(
            residual_body, "residual", (jnp.bfloat16,), *sums, targets, earlier=tangent_terms
        )
        tangent_sums = self.sums(tangent_terms, (piece,))

        def tangent(*earlier):
            (tangent_piece,) = by_rows(
                tangent_body, "tangent_res", (jnp.bfloat16,), *tangent_sums, earlier=earlier
            )
            return tangent_piece, both_halves(tangent_piece)

        return both_halves(piece), tangent


class Gathers:
    def whole(self, rows):
        return lax.all_gather(rows, "tensor", axis=0, tiled=True)

    def inputs(self, tokens, targets):
        return self.whole(tokens), targets

    def residuals(self, term, hidden, tangent_hidden, targets, earlier):
        first, second = (
            lax.psum_scatter(term(source), "tensor", scatter_dimension=0, tiled=True)
            for source in (hidden, tangent_hidden)
        )
        residual = (first - targets.astype(jnp.float32)).astype(jnp.bfloat16)
        tangent_piece = second.astype(jnp.bfloat16)
        return self.whole(residual), lambda *earlier: (tangent_piece, self.whole(tangent_piece))


def ring_order(count):
    if count == 8:
        return [0, 2, 4, 6, 7, 5, 3, 1]
    return list(range(count))


def ring_gather(block, axis):
    count = lax.axis_size("replica")
    order = ring_order(count)
    onward = [(order[i], order[(i + 1) % count]) for i in range(count)]
    back = [(b, a) for a, b in onward]
    place = [0] * count
    for at, replica in enumerate(order):
        place[replica] = at
    here = jnp.array(place, jnp.int32)[lax.axis_index("replica")]
    owner = jnp.array(order, jnp.int32)
    extent = block.shape[axis]
    shape = list(block.shape)
    shape[axis] = extent * count
    whole = blank(tuple(shape), block.dtype)

    def put(whole, piece, step, start=0):
        at = owner[jnp.mod(here + step, count)] * extent + start
        index = [0] * block.ndim
        index[axis] = at
        return lax.dynamic_update_slice(whole, piece, index)

    whole = put(whole, block, 0)
    ahead = behind = block
    full_steps = (count - 1) // 2
    first_block = block
    for step in range(1, full_steps + 1):
        ahead = send(ahead, onward)
        behind = send(behind, back)
        if step == 1:
            first_block = ahead
        whole = put(whole, ahead, -step)
        whole = put(whole, behind, step)
    if count % 2 == 0:
        half = extent // 2
        first = lax.slice_in_dim(ahead, 0, half, axis=axis)
        second = lax.slice_in_dim(behind, half, extent, axis=axis)
        whole = put(whole, send(first, onward), -(full_steps + 1))
        whole = put(whole, send(second, back), full_steps + 1, half)
    return whole, first_block


def link_matrix(neighbours, numerators):
    count = neighbours.shape[0]
    ids = jnp.arange(count, dtype=neighbours.dtype)
    listed = jnp.sum(
        jnp.where(neighbours[:, :, None] == ids[None, None, :], numerators[:, :, None], 0), axis=1
    )
    own = DEN - jnp.sum(numerators, axis=1)
    return (listed + jnp.diag(own)).astype(jnp.float32) / DEN


class Grid:
    outer = [(2 * a + x, 2 * b + x) for a, b in ((0, 1), (1, 0), (2, 3), (3, 2)) for x in (0, 1)]
    inner = [(2 * a + x, 2 * b + x) for a, b in ((1, 2), (2, 1)) for x in (0, 1)]
    across = [(2 * z + x, 2 * z + 1 - x) for z in range(4) for x in (0, 1)]

    @staticmethod
    def picks():
        found = np.zeros((8, 10, 8, 8), np.float32)
        for r in range(8):
            z, x = divmod(r, 2)
            inside = z in (1, 2)
            swapped = 2 * (z ^ 1) + x
            middle = 2 * (3 - z) + x
            far = (6 if z == 1 else 0) + x
            other = 2 * z + 1 - x
            edge = (0 if z == 1 else 6) + x
            found[r, 0, r, r] = found[r, 1, r, swapped] = 1
            found[r, 4, other, r] = found[r, 5, other, swapped] = 1
            if inside:
                found[r, 2, r, middle] = found[r, 3, r, far] = 1
                found[r, 6, other, middle] = 1
                found[r, 7, edge, middle] = found[r, 8, edge, far] = 1
        found[2, 9, 0, 7] = found[5, 9, 7, 0] = 1
        return found


STEPS = 2


def tick_kernel(plan, inv_width, *refs):
    names, results = plan
    got = dict(zip(names + results, refs))
    scale_ref = got["scales"]

    def weighted(first, *parts):
        total = None
        for k, part in enumerate(parts):
            term = scale_ref[first + k] * got[part][...].astype(jnp.float32)
            total = term if total is None else total + term
        return total

    put = {}
    if "grads" in got:
        slope = (
            jnp.dot(got["tokens_t"][...], got["grads"][...], preferred_element_type=jnp.float32)
            * inv_width
        )
        base = got["base"][...].astype(jnp.float32)
        tracked = got["tracker"][...].astype(jnp.float32)
        if "step" in names:
            ratio = slope / jnp.maximum(tracked, floor_value)
            made = base - step_size * jnp.clip(ratio, -1.0, 1.0)
        else:
            made = tracker_decay * tracked + (1.0 - tracker_decay) * base * slope
        put["made"] = made.astype(jnp.bfloat16)
    if "cross_own" in got:
        put["cross"] = weighted(4, "cross_own", "cross_swapped", "cross_middle").astype(jnp.bfloat16)
    if "pass_swapped" in got:
        put["pass_swapped"] = got["pass_swapped"][...]
    if "pass_far" in got:
        put["pass_far"] = got["pass_far"][...]
    if "out_middle" in got:
        put["outward"] = weighted(7, "out_middle", "out_far", "out_wrapped").astype(jnp.bfloat16)
    step = pl.program_id(0)
    for result in results:
        if result != "mixed":
            offset = 0
            for at, piece in enumerate(result.split(":")[1].split("+")):
                if len(got[result].shape) == 3:
                    got[result][at] = put[piece]
                    continue
                rows = put[piece].shape[0]
                start = pl.multiple_of(offset + step * rows, rows)
                got[result][pl.ds(start, rows), :] = put[piece]
                offset += rows * STEPS
    if "mixed" in got:
        total = weighted(0, "own", "swapped", "middle", "far")
        total = total + got["sideways"][...].astype(jnp.float32)
        got["mixed"][...] = (total + got["rest"][...].astype(jnp.float32)).astype(jnp.bfloat16)


class Pipeline:
    def __init__(self, scales, full_rows, width):
        self.scales = scales
        self.full_rows, self.width = full_rows, width
        self.place = {}
        self.received = {}
        self.last = None

    def parts(self, count):
        unit = self.full_rows // 64
        sizes = [[4] * 16 for _ in range(count)]
        sizes[0] = [4] * 16
        sizes[-1] = [4] * 15 + [2] * 2
        found = []
        for which, units in enumerate(sizes):
            row = 0
            for size in units:
                found.append((which, row, size * unit))
                row += size * unit
        return found

    def run(self, stepping, tracking):
        self.sources = [(*stepping, "step"), None]
        self.before = {}
        self.order = self.parts(2)
        self.mixed = [None, None]
        for tick in range(len(self.order) + 7):
            if tick == 3:
                tracked, (first, second) = tracking(self.last)
                self.sources[1] = (*tracked, "track")
                self.before = {6: [first], 9: [second]}
            self.kernel(("outer", "inner"), tick)
            self.kernel(("across",), tick)
        return self.mixed

    def kernel(self, ways, tick):
        width, parts, place, mixed = self.width, self.order, self.place, self.mixed
        count = len(parts)
        names, operands, specs = ["scales"], [self.scales], [pl.BlockSpec(memory_space=pltpu.SMEM)]

        def row_spec(depth, start, rows):
            block = rows // STEPS
            assert start % block == 0
            return pl.BlockSpec((block, depth), lambda i: (start // block + i, 0))

        def add(name, key):
            array, start = place[key]
            rows = parts[key[1]][2]
            names.append(name)
            operands.append(array)
            if array.ndim == 3:
                item = start // rows
                specs.append(pl.BlockSpec((None, rows // STEPS, width), lambda i: (item, i, 0)))
            else:
                specs.append(row_spec(width, start, rows))

        def add_earlier(array):
            names.append("earlier")
            operands.append(array)
            specs.append(pl.BlockSpec(memory_space=pl.ANY))

        payloads = {way: [] for way in ways}
        flops = moved = 0
        if "inner" in ways:
            part = tick
            if part < count:
                which, start, rows = parts[part]
                tokens_t, grads, base, tracker, kind = self.sources[which]
                depth = grads.shape[0]
                names += ["tokens_t", "grads", "base", "tracker", kind]
                operands += [tokens_t, grads, base, tracker, self.scales]
                specs += [
                    row_spec(depth, start, rows),
                    pl.BlockSpec((depth, width), lambda i: (0, 0)),
                    row_spec(width, start, rows),
                    row_spec(width, start, rows),
                    pl.BlockSpec(memory_space=pltpu.SMEM),
                ]
                payloads["outer"].append(("made", "swapped", part))
                payloads["inner"].append(("made", "middle", part))
                flops += 2 * rows * depth * width
                moved += 2 * rows
            part = tick - 2
            if 0 <= part < count:
                add("pass_swapped", ("swapped", part))
                payloads["inner"].append(("pass_swapped", "far", part))
            part = tick - 5
            if 0 <= part < count:
                add("out_middle", ("middle", part))
                add("out_far", ("far", part))
                add("out_wrapped", ("wrapped", part))
                payloads["outer"].append(("outward", "rest", part))
                moved += 2 * parts[part][2]
            for array in self.before.get(tick, ()):
                add_earlier(array)
        else:
            part = tick - 2
            if 0 <= part < count:
                add("cross_own", ("own", part))
                add("cross_swapped", ("swapped", part))
                add("cross_middle", ("middle", part))
                payloads["across"].append(("cross", "sideways", part))
                moved += 2 * parts[part][2]
            part = tick - 3
            if 0 <= part < count:
                add("pass_far", ("far", part))
                payloads["across"].append(("pass_far", "wrapped", part))
            if ("inner", tick - 1) in self.received:
                add_earlier(self.received["inner", tick - 1])
        results, shapes, out_specs = [], [], []
        ways = [way for way, pieces in payloads.items() if pieces]
        for way in ways:
            payloads[way].sort(key=lambda piece: -parts[piece[2]][2])
            rows = sum(parts[piece[2]][2] for piece in payloads[way])
            moved += 2 * rows
            results.append(way + ":" + "+".join(piece[0] for piece in payloads[way]))
            sizes = {parts[piece[2]][2] for piece in payloads[way]}
            if len(sizes) == 1:
                items, each = len(payloads[way]), sizes.pop()
                shapes.append(jax.ShapeDtypeStruct((items, each, width), jnp.bfloat16))
                out_specs.append(pl.BlockSpec((items, each // STEPS, width), lambda i: (0, i, 0)))
            else:
                shapes.append(jax.ShapeDtypeStruct((rows, width), jnp.bfloat16))
                out_specs.append(pl.BlockSpec((rows, width), lambda i: (0, 0)))
        aliases = {}
        part = tick - 7
        mixing = 0 <= part < count and "inner" not in payloads
        if mixing:
            for name in ("own", "swapped", "middle", "far", "sideways", "rest"):
                add(name, (name, part))
            which, start, rows = parts[part]
            if mixed[which] is not None:
                aliases = {len(operands): len(results)}
                names.append("target")
                operands.append(mixed[which])
                specs.append(pl.BlockSpec(memory_space=pl.ANY))
            moved += 7 * rows
            results.append("mixed")
            shapes.append(jax.ShapeDtypeStruct((self.full_rows, width), jnp.bfloat16))
            out_specs.append(row_spec(width, start, rows))
        if not results:
            return
        if self.last is not None:
            add_earlier(self.last)
        got = pl.pallas_call(
            functools.partial(
                tick_kernel, (tuple(names), tuple(results)), 1.0 / math.sqrt(self.full_rows)
            ),
            grid=(STEPS,),
            in_specs=specs,
            out_specs=out_specs,
            out_shape=shapes,
            input_output_aliases=aliases,
            compiler_params=pltpu.CompilerParams(vmem_limit_bytes=TICK_VMEM_BYTES),
            cost_estimate=pl.CostEstimate(
                flops=flops, bytes_accessed=2 * moved * width, transcendentals=0
            ),
            name="tick_across" if mixing or "across" in ways else "tick",
        )(*operands)
        if mixing:
            mixed[which] = got[-1]
        for way, payload in zip(ways, got):
            self.last = payload
            received = send(payload, getattr(Grid, way))
            self.received[way, tick] = received
            start = 0
            for _, name, part in payloads[way]:
                place[name, part] = (received, start)
                if name == "swapped":
                    place["own", part] = (payload, start)
                start += parts[part][2]


class OffsetMixer:
    offsets = (1, -1, 2, -2, 4, -4)

    def __init__(self, links):
        count = lax.axis_size("replica")
        me = lax.axis_index("replica")
        self.steps = sorted({offset % count for offset in self.offsets})
        columns = jnp.stack([me] + [jnp.mod(me - step, count) for step in self.steps])
        self.scales = links[me][columns]
        self.pairs = [[(s, (s + step) % count) for s in range(count)] for step in self.steps]

    def mix(self, part):
        parts = [part] + [send(part, pairs) for pairs in self.pairs]
        return weighted_sum("mixed_rows", self.scales, parts)


def local(
    tokens, targets, gate_weight, probes, tracker, up_weight, down_weight, neighbours, numerators
):
    weight_now = gate_weight[0]
    tracker_now = tracker[0]
    probe_here = probes[0]
    width = weight_now.shape[0]
    hidden_units = down_weight.shape[0] * lax.axis_size("tensor")
    inv_width = 1.0 / math.sqrt(width)
    inv_hidden = 1.0 / math.sqrt(hidden_units)

    links = link_matrix(neighbours, numerators)

    group = Swaps() if lax.axis_size("tensor") == 4 else Gathers()
    gathered, target_rows = group.inputs(tokens[0], targets[0])
    gathered_t = turned(gathered)
    scales = jnp.zeros(1)
    if lax.axis_size("replica") == 8:
        scales = jnp.sum(
            jnp.asarray(Grid.picks())[lax.axis_index("replica")] * links, axis=(1, 2)
        )
    up_full, first_block = ring_gather(up_weight, 0)
    down_full, _ = ring_gather(after(down_weight, first_block, target_rows, gathered_t, scales), 1)

    gate_pre = jnp.dot(gathered, weight_now, preferred_element_type=jnp.float32) * inv_width
    probe_pre = jnp.dot(gathered, probe_here, preferred_element_type=jnp.float32) * inv_width
    up_pre = jnp.dot(gathered, up_full, preferred_element_type=jnp.float32) * inv_width
    logistic = jax.nn.sigmoid(gate_pre)
    activated = gate_pre * logistic
    slope_one = logistic * (1.0 + gate_pre * (1.0 - logistic))
    slope_two = logistic * (1.0 - logistic) * (2.0 + gate_pre * (1.0 - 2.0 * logistic))
    hidden = (activated * up_pre).astype(jnp.bfloat16)
    gate_factor = up_pre * slope_one
    curve_factor = slope_two * probe_pre * up_pre
    tangent_hidden = (slope_one * probe_pre * up_pre).astype(jnp.bfloat16)

    def forward_term(source):
        return jnp.dot(source, down_full, preferred_element_type=jnp.float32) * inv_hidden

    residual, tangent_sums = group.residuals(
        forward_term, hidden, tangent_hidden, target_rows, (gate_factor, curve_factor)
    )
    grad_hidden, grad_gate = backward(
        gate_body,
        "backward_gate",
        inv_hidden,
        (jnp.float32, jnp.bfloat16),
        residual,
        down_full,
        gate_factor,
    )

    def tracking(*earlier):
        tangent_piece, tangent_res = tangent_sums(*earlier)
        (tangent_gate,) = backward(
            tangent_gate_body,
            "tangent_gate",
            inv_hidden,
            (jnp.bfloat16,),
            tangent_res,
            down_full,
            gate_factor,
            grad_hidden,
            curve_factor,
        )
        return (gathered_t, tangent_gate, probe_here, tracker_now), (tangent_piece, tangent_gate)

    stepping = (gathered_t, grad_gate, weight_now, tracker_now)
    if lax.axis_size("replica") == 8:
        pipeline = Pipeline(scales, width, weight_now.shape[1])
        mixed_weights, mixed_tracker = pipeline.run(stepping, tracking)
    else:
        mixer = OffsetMixer(links)
        mixed_weights = mixer.mix(update_rows(step_body, "stepped_rows", *stepping))
        mixed_tracker = mixer.mix(update_rows(track_body, "tracked_rows", *tracking()[0]))
    return (mixed_weights[None], mixed_tracker[None])


def solution(mesh):
    return jax.shard_map(
        local,
        mesh=mesh,
        in_specs=(
            P("replica", "tensor", None),
            P("replica", "tensor", None),
            P("replica", None, "tensor"),
            P("replica", None, "tensor"),
            P("replica", None, "tensor"),
            P("replica", "tensor"),
            P("tensor", "replica"),
            P(),
            P(),
        ),
        out_specs=(P("replica", None, "tensor"), P("replica", None, "tensor")),
        check_vma=False,
    )
```
